32 devices in a mesh: seq: 16 (over z, y, core), mp: 2 (over x).
Axes of the slice: x: 2, y: 2, z: 4, core: 2. Of those that a mesh axis runs over, the one named last changes fastest.
Arguments:
- tokens: bfloat16 [4096, 4096], P('seq', 'mp'), may hold values from -16 to 16
- grad_out: bfloat16 [4096, 4096], P('seq', 'mp'), may hold values from -6 to 6
- w_query: bfloat16 [4096, 4096], P('seq', 'mp'), may hold values from -0.09375 to 0.09375
- w_key: bfloat16 [4096, 1024], P('seq', 'mp'), may hold values from -0.09375 to 0.09375
- w_value: bfloat16 [4096, 1024], P('seq', 'mp'), may hold values from -0.09375 to 0.09375
- doc_lengths: int32 [4], replicated, may hold values from 1 to 24, 32 in all
Outputs:
- grad_tokens: bfloat16 [4096, 4096], P('seq', 'mp')
- grad_w_query: float32 [4096, 4096], P('seq', 'mp')
- grad_w_key: float32 [4096, 1024], P('seq', 'mp')
- grad_w_value: float32 [4096, 1024], P('seq', 'mp')
The draws below stay inside these ranges and needn't reach their ends.
Inputs may be any that keep to these rules, and one draw needn't show every extreme that they name: `doc_lengths`: the lengths sum to 32.
All inputs are finite; a program needn't handle non-finite values.
Results may differ from the reference program's by a relative error of at most 0.03.
The reference program's roundings to bfloat16 on the way (of `query`, `probs_low` and `grad_scores`) count: a program that leaves them out, or rounds other values in their place, can miss the bound.
Values may be sent and summed in bfloat16 or wider, within the bound.
A program may use at most 128 MiB of HBM per device.

```python
import math
import jax
import jax.numpy as jnp
import numpy as np
from jax import lax

D = 4096
HEADS = 32
KV_HEADS = 8
HEAD_DIM = 128
WINDOW = 4096
TOK_DEV = 256
ALIGN = 128
DOCS = 4
LIST = 4096
KV_DIM = 1024
TOTAL_BLOCKS = 32
MOST_BLOCKS = 24
N_SEQ = 16


def draw_tokens(key, part):
    first_key = jax.random.fold_in(key, 0)
    base = jax.random.normal(first_key, (LIST, D), jnp.float32)
    values = base
    return jnp.clip(values, -16.0, 16.0).astype(jnp.bfloat16)


def steps_of(stream_key, dims, cuts, smallest, top_value):
    loudness = 1.0
    for dim, blocks in cuts:
        draws = jax.random.uniform(jax.random.fold_in(jax.random.fold_in(stream_key, 6), dim), (blocks,), jnp.float32, smallest / len(cuts), top_value / len(cuts))
        loudness = loudness * jnp.repeat(jnp.exp(draws), dims[dim] // blocks).reshape((-1,) + (1,) * (len(dims) - 1 - dim))
    return loudness


def split_up(number_of, total, bound, slope):
    portions = [(1 << 20) // math.isqrt(grade ** slope) + 1 for grade in range(2, number_of + 1)]
    rest, given = total - bound - (number_of - 1), [1] * (number_of - 1)
    while rest > 0:
        free = [i for i in range(number_of - 1) if given[i] < bound]
        pool, remaining = sum([portions[i] for i in free]), rest
        for i in free:
            extra = min(bound - given[i], max(1, remaining * portions[i] // pool), rest)
            given[i] = given[i] + extra
            rest = rest - extra
    return np.array([bound] + given)


def uneven_parts(own_key, amount, total, most, skew):
    if amount == 2:
        one = jax.random.randint(own_key, (), max(1, total - most), min(most, total - 1) + 1)
        return jnp.stack([one, total - one])
    sizes = jnp.asarray(split_up(amount, total, most, skew), jnp.int32)
    pairs = (amount - 1) // 2
    donor, taker = sizes[1:1 + 2 * pairs:2], sizes[2:2 + 2 * pairs:2]
    slack = jnp.minimum(donor - 1, most - taker)
    passed = jax.random.randint(jax.random.fold_in(own_key, 1), (pairs,), 0, 1 << 20) % (slack + 1)
    sizes = sizes.at[1:1 + 2 * pairs:2].set(donor - passed).at[2:2 + 2 * pairs:2].set(taker + passed)
    return sizes[jax.random.permutation(jax.random.fold_in(own_key, 2), amount)]


def centred(stream_key, dims, deviation, limit, shards=(), kind=jnp.bfloat16):
    array = jax.random.normal(stream_key, dims, jnp.float32) * deviation
    if len(shards) > 0:
        array = steps_of(stream_key, dims, shards, -0.22, 0.18) * array
    return jnp.clip(array, min=-limit, max=limit).astype(kind)


def setup_inputs(seed: int = 0) -> dict:
    splits = jax.random.split(jax.random.key(seed), 7)
    tokens = draw_tokens(jax.random.fold_in(splits[6], 71), 0)
    grad_out = centred(splits[1], (LIST, D), 1.0, 6.0, ((0, 16), (1, 2)))
    w_query = centred(splits[2], (D, D), D ** -0.5, 0.09375, ((0, 16), (1, 2)))
    w_key = centred(splits[3], (D, KV_DIM), D ** -0.5, 0.09375, ((0, 16), (1, 2)))
    w_value = centred(splits[4], (D, KV_DIM), D ** -0.5, 0.09375, ((0, 16), (1, 2)))
    doc_lengths = uneven_parts(splits[5], DOCS, TOTAL_BLOCKS, MOST_BLOCKS, 2).astype(jnp.int32)
    return dict(tokens=tokens, grad_out=grad_out, w_query=w_query, w_key=w_key, w_value=w_value, doc_lengths=doc_lengths)


THETA = 10000.0


def list_offsets(positions, ends, lengths):
    after = positions[:, None] >= ends[None, :]
    member = jnp.sum(after.astype(jnp.int32), axis=1).astype(jnp.int32)
    before = jnp.sum(jnp.where(after, lengths[None, :] * ALIGN, 0), axis=1).astype(jnp.int32)
    return member, (positions - before).astype(jnp.int32)


def rope_tables(offsets):
    half = HEAD_DIM // 2
    inverse = THETA ** (-(jnp.arange(half, dtype=jnp.float32) * 2.0 / HEAD_DIM))
    angle = offsets.astype(jnp.float32)[:, None] * inverse[None, :]
    angle = jnp.concatenate([angle, angle], axis=1)
    return jnp.cos(angle), jnp.sin(angle)


def rotate(vectors, cosine, sine, direction):
    half = vectors.shape[-1] // 2
    turned = jnp.concatenate([-vectors[..., half:], vectors[..., :half]], axis=-1)
    return vectors * cosine[:, None, :] + direction * turned * sine[:, None, :]


def reference(tokens, grad_out, w_query, w_key, w_value, doc_lengths):
    group = HEADS // KV_HEADS
    scale = HEAD_DIM ** -0.5
    ends = (jnp.cumsum(doc_lengths) * ALIGN).astype(jnp.int32)
    positions = jnp.arange(LIST, dtype=jnp.int32)
    member, offsets = list_offsets(positions, ends, doc_lengths)
    cosine, sine = rope_tables(offsets)
    query = rotate(jnp.dot(tokens, w_query, preferred_element_type=jnp.float32).reshape(LIST, HEADS, HEAD_DIM), cosine, sine, 1.0)
    query = query.astype(jnp.bfloat16).reshape(LIST, KV_HEADS, group, HEAD_DIM)
    keys = rotate(jnp.dot(tokens, w_key, preferred_element_type=jnp.float32).reshape(LIST, KV_HEADS, HEAD_DIM), cosine, sine, 1.0)
    keys = keys.astype(jnp.bfloat16)
    values = jnp.dot(tokens, w_value, preferred_element_type=jnp.float32).astype(jnp.bfloat16).reshape(LIST, KV_HEADS, HEAD_DIM)
    grad_heads = grad_out.reshape(LIST, KV_HEADS, group, HEAD_DIM)
    front = jnp.zeros((WINDOW, KV_HEADS, HEAD_DIM), jnp.bfloat16)
    keys_pad = jnp.concatenate([front, keys], axis=0)
    values_pad = jnp.concatenate([front, values], axis=0)
    member_pad = jnp.concatenate([-jnp.ones((WINDOW,), jnp.int32), member], axis=0)
    reach = WINDOW + TOK_DEV

    def one_block(carry, index):
        key_acc, value_acc = carry
        start = (index * TOK_DEV).astype(jnp.int32)
        query_block = lax.dynamic_slice_in_dim(query, start, TOK_DEV, 0).astype(jnp.float32)
        grad_block = lax.dynamic_slice_in_dim(grad_heads, start, TOK_DEV, 0).astype(jnp.float32)
        key_block = lax.dynamic_slice_in_dim(keys_pad, start, reach, 0).astype(jnp.float32)
        value_block = lax.dynamic_slice_in_dim(values_pad, start, reach, 0).astype(jnp.float32)
        query_pos = start + jnp.arange(TOK_DEV, dtype=jnp.int32)
        key_pos = start - WINDOW + jnp.arange(reach, dtype=jnp.int32)
        query_member = lax.dynamic_slice_in_dim(member, start, TOK_DEV, 0)
        key_member = lax.dynamic_slice_in_dim(member_pad, start, reach, 0)
        gap = query_pos[:, None] - key_pos[None, :]
        live = (gap >= 0) & (gap < WINDOW) & (query_member[:, None] == key_member[None, :])
        scores = jnp.einsum("qagd,kad->agqk", query_block, key_block) * scale
        scores = jnp.where(live, scores, -jnp.inf)
        top = jnp.max(scores, axis=-1, keepdims=True)
        weights = jnp.exp(scores - top)
        probs = weights / jnp.sum(weights, axis=-1, keepdims=True)
        probs_low = lax.optimization_barrier(probs.astype(jnp.bfloat16)).astype(jnp.float32)
        attended = jnp.einsum("agqk,kad->qagd", probs_low, value_block)
        delta = jnp.sum(grad_block * attended, axis=-1)
        grad_probs = jnp.einsum("qagd,kad->agqk", grad_block, value_block)
        grad_scores = probs * (grad_probs - jnp.transpose(delta, (1, 2, 0))[..., None])
        grad_scores = lax.optimization_barrier(grad_scores.astype(jnp.bfloat16)).astype(jnp.float32)
        grad_query = scale * jnp.einsum("agqk,kad->qagd", grad_scores, key_block)
        grad_keys = scale * jnp.einsum("agqk,qagd->kad", grad_scores, query_block)
        grad_values = jnp.einsum("agqk,qagd->kad", probs_low, grad_block)
        key_acc = lax.dynamic_update_slice_in_dim(key_acc, lax.dynamic_slice_in_dim(key_acc, start, reach, 0) + grad_keys, start, 0)
        value_acc = lax.dynamic_update_slice_in_dim(value_acc, lax.dynamic_slice_in_dim(value_acc, start, reach, 0) + grad_values, start, 0)
        return (key_acc, value_acc), grad_query

    empty = jnp.zeros((LIST + WINDOW, KV_HEADS, HEAD_DIM), jnp.float32)
    (key_acc, value_acc), query_grads = lax.scan(one_block, (empty, empty), jnp.arange(LIST // TOK_DEV, dtype=jnp.int32))
    dquery = query_grads.reshape(LIST, HEADS, HEAD_DIM)
    grad_query = rotate(dquery, cosine, sine, -1.0).astype(jnp.bfloat16).reshape(LIST, D)
    grad_key = rotate(key_acc[WINDOW:], cosine, sine, -1.0).astype(jnp.bfloat16).reshape(LIST, KV_DIM)
    grad_value = value_acc[WINDOW:].astype(jnp.bfloat16).reshape(LIST, KV_DIM)
    grad_all = jnp.concatenate([grad_query, grad_key, grad_value], axis=1)
    weights_all = jnp.concatenate([w_query, w_key, w_value], axis=1)
    grad_tokens = lax.dot_general(grad_all, weights_all, (((1,), (1,)), ((), ())), preferred_element_type=jnp.float32).astype(jnp.bfloat16)

    def weight_block(total, index):
        start = (index * TOK_DEV).astype(jnp.int32)
        rows_block = lax.dynamic_slice_in_dim(tokens, start, TOK_DEV, 0)
        grads_block = lax.dynamic_slice_in_dim(grad_all, start, TOK_DEV, 0)
        part = lax.dot_general(rows_block, grads_block, (((0,), (0,)), ((), ())), preferred_element_type=jnp.float32)
        part = lax.optimization_barrier(part.astype(jnp.bfloat16))
        return total + part.astype(jnp.float32), None

    total, _ = lax.scan(weight_block, jnp.zeros((D, D + 2 * KV_DIM), jnp.float32), jnp.arange(N_SEQ, dtype=jnp.int32))
    return (grad_tokens, total[:, :D], total[:, D:D + KV_DIM], total[:, D + KV_DIM:])
```

```python
import functools

import jax
import jax.numpy as jnp
from jax import lax
from jax.experimental import pallas as pl
from jax.experimental.pallas import tpu as pltpu
from jax.sharding import PartitionSpec as P

HEAD_DIM = 128
WINDOW = 4096
ALIGN = 128
THETA = 10000.0
KEY_BLOCK = 256
LOG2E = 1.4426950408889634
CONTRACT_LAST = (((1,), (1,)), ((), ()))
CONTRACT_FIRST = (((0,), (0,)), ((), ()))


def list_starts(positions, lengths):
    start = jnp.zeros_like(positions)
    end = jnp.int32(0)
    for k in range(lengths.shape[0]):
        end = end + lengths[k] * ALIGN
        start = jnp.where(positions >= end, end, start)
    return start


def rope_tables(offsets):
    half = HEAD_DIM // 2
    inverse = THETA ** (-(jnp.arange(half, dtype=jnp.float32) * 2.0 / HEAD_DIM))
    angle = offsets.astype(jnp.float32)[:, None] * inverse[None, :]
    cosine, sine = jnp.cos(angle), jnp.sin(angle)
    return (
        jnp.concatenate([cosine, cosine], axis=1),
        jnp.concatenate([-sine, sine], axis=1),
    )


def rotate(flat, cosine, sine, direction):
    half = HEAD_DIM // 2
    out = []
    for h in range(flat.shape[1] // HEAD_DIM):
        v = flat[:, h * HEAD_DIM : (h + 1) * HEAD_DIM]
        turned = jnp.concatenate([v[:, half:], v[:, :half]], axis=1)
        out.append(v * cosine + direction * turned * sine)
    return jnp.concatenate(out, axis=1)


def attention_kernel(
    group, scale, span_ref, q_ref, go_ref, k_ref, v_ref, cos_ref, sin_ref, low_ref, pos_ref,
    dq_ref, dk_ref, dv_ref, score_ref, gprob_ref, dqt_ref,
):
    half = HEAD_DIM // 2
    kb = KEY_BLOCK
    rows = q_ref.shape[0]
    cols = group * rows
    first_block, blocks = span_ref[0], span_ref[1]
    cosine, sine = cos_ref[...], sin_ref[...]

    def head(ref, h):
        return ref[:, h * HEAD_DIM : (h + 1) * HEAD_DIM]

    query = jnp.concatenate(
        [
            (head(q_ref, h) * cosine + pltpu.roll(head(q_ref, h), half, 1) * sine).astype(jnp.bfloat16)
            for h in range(group)
        ],
        axis=0,
    )
    grads = jnp.concatenate([head(go_ref, h) for h in range(group)], axis=0)
    low = jnp.concatenate([low_ref[...]] * group, axis=1)
    pos = jnp.concatenate([pos_ref[...]] * group, axis=1)
    dk_ref[...] = jnp.zeros_like(dk_ref)
    dv_ref[...] = jnp.zeros_like(dv_ref)
    dqt_ref[...] = jnp.zeros_like(dqt_ref)

    def rows_of(i):
        return pl.ds(pl.multiple_of((first_block + i) * kb, kb), kb)

    def fold(x, op):
        x = x.reshape(kb // 8, 8, cols)
        return op(x, axis=0)

    def score_step(i, top):
        s = lax.dot_general(
            k_ref[rows_of(i), :], query, CONTRACT_LAST, preferred_element_type=jnp.float32
        ) * (scale * LOG2E)
        kpos = (first_block + i) * kb + lax.broadcasted_iota(jnp.int32, (kb, cols), 0)
        s = jnp.where((kpos <= pos) & (kpos >= low), s, -jnp.inf)
        score_ref[i] = s
        return jnp.maximum(top, fold(s, jnp.max))

    top = lax.fori_loop(0, blocks, score_step, jnp.full((8, cols), -jnp.inf, jnp.float32))
    top = jnp.max(top, axis=0, keepdims=True)

    def mass_step(i, mass):
        e = jnp.exp2(score_ref[i] - top)
        score_ref[i] = e
        gprob_ref[i] = lax.dot_general(
            v_ref[rows_of(i), :], grads, CONTRACT_LAST, preferred_element_type=jnp.float32
        )
        return mass + fold(e, jnp.sum)

    mass = lax.fori_loop(0, blocks, mass_step, jnp.zeros((8, cols), jnp.float32))
    inverse = 1.0 / jnp.sum(mass, axis=0, keepdims=True)

    def delta_step(i, delta):
        low_probs = (score_ref[i] * inverse).astype(jnp.bfloat16)
        dv_ref[rows_of(i), :] = jnp.dot(
            low_probs, grads, preferred_element_type=jnp.float32
        ).astype(dv_ref.dtype)
        return delta + fold(low_probs.astype(jnp.float32) * gprob_ref[i], jnp.sum)

    delta = lax.fori_loop(0, blocks, delta_step, jnp.zeros((8, cols), jnp.float32))
    delta = jnp.sum(delta, axis=0, keepdims=True)

    def grad_step(i, carry):
        g = (score_ref[i] * inverse * (gprob_ref[i] - delta)).astype(jnp.bfloat16)
        dk_ref[rows_of(i), :] = (
            jnp.dot(g, query, preferred_element_type=jnp.float32) * scale
        ).astype(dk_ref.dtype)
        dqt_ref[...] += lax.dot_general(
            k_ref[rows_of(i), :], g, CONTRACT_FIRST, preferred_element_type=jnp.float32
        )
        return carry

    lax.fori_loop(0, blocks, grad_step, 0)
    for h in range(group):
        d = dqt_ref[:, h * rows : (h + 1) * rows].T * scale
        d = d * cosine - pltpu.roll(d, half, 1) * sine
        dq_ref[:, h * HEAD_DIM : (h + 1) * HEAD_DIM] = d.astype(dq_ref.dtype)


def attention(span, query, grad_out, keys_values, cosine, sine, low, pos):
    rows, head_cols = query.shape
    length, kv_cols = keys_values.shape[0], keys_values.shape[1] // 2
    kv_here = kv_cols // HEAD_DIM
    group = head_cols // kv_cols
    wide = group * HEAD_DIM
    cols = group * rows
    slots = min(length, WINDOW + rows) // KEY_BLOCK
    whole = lambda shape: pl.BlockSpec(shape, lambda g, s: (0, 0))
    column = pl.BlockSpec((length, HEAD_DIM), lambda g, s: (0, g))
    heads = pl.BlockSpec((rows, wide), lambda g, s: (0, g))
    return pl.pallas_call(
        functools.partial(attention_kernel, group, HEAD_DIM ** (-0.5)),
        grid_spec=pltpu.PrefetchScalarGridSpec(
            num_scalar_prefetch=1,
            grid=(kv_here,),
            in_specs=[
                heads,
                heads,
                column,
                pl.BlockSpec((length, HEAD_DIM), lambda g, s: (0, g + kv_here)),
                whole((rows, HEAD_DIM)),
                whole((rows, HEAD_DIM)),
                whole((1, rows)),
                whole((1, rows)),
            ],
            out_specs=[heads, column, column],
            scratch_shapes=[
                pltpu.VMEM((slots, KEY_BLOCK, cols), jnp.float32),
                pltpu.VMEM((slots, KEY_BLOCK, cols), jnp.float32),
                pltpu.VMEM((HEAD_DIM, cols), jnp.float32),
            ],
        ),
        out_shape=[
            jax.ShapeDtypeStruct((rows, head_cols), jnp.bfloat16),
            jax.ShapeDtypeStruct((length, kv_cols), jnp.bfloat16),
            jax.ShapeDtypeStruct((length, kv_cols), jnp.bfloat16),
        ],
        compiler_params=pltpu.CompilerParams(vmem_limit_bytes=58 * 1024 * 1024),
        cost_estimate=pl.CostEstimate(
            flops=6 * rows * length * head_cols,
            bytes_accessed=8 * length * kv_cols,
            transcendentals=rows * length * head_cols // HEAD_DIM,
        ),
    )(span, query, grad_out, keys_values, keys_values, cosine, sine, low, pos)


def local(tokens, grad_out, w_query, w_key, w_value, doc_lengths):
    rows = tokens.shape[0]
    head_cols = w_query.shape[1]
    kv_cols = w_key.shape[1]
    first = lax.axis_index("seq") * rows
    pos = first + jnp.arange(rows, dtype=jnp.int32)
    start = list_starts(pos, doc_lengths)
    cosine, sine = rope_tables(pos - start)
    low = jnp.maximum(start, pos - (WINDOW - 1))
    first_block = low[0] // KEY_BLOCK
    blocks = (first + rows - 1) // KEY_BLOCK - first_block + 1
    span = jnp.stack([first_block, blocks]).astype(jnp.int32)

    whole = lax.all_gather(tokens, "mp", axis=1, tiled=True)
    w_kv = lax.all_gather(
        jnp.concatenate([w_key, w_value], axis=1), "seq", axis=0, tiled=True
    )
    w_q = lax.all_gather(w_query, "seq", axis=0, tiled=True)
    kv = jnp.dot(whole, w_kv, preferred_element_type=jnp.float32)
    keys_values = jnp.concatenate(
        [rotate(kv[:, :kv_cols], cosine, sine, 1.0).astype(jnp.bfloat16), kv[:, kv_cols:].astype(jnp.bfloat16)],
        axis=1,
    )
    keys_values = lax.all_gather(keys_values, "seq", axis=0, tiled=True)
    query = jnp.dot(whole, w_q, preferred_element_type=jnp.float32)

    grad_query, dkeys, dvalues = attention(
        span, query, grad_out, keys_values, cosine, sine, low[None], pos[None]
    )
    key_grad = lax.psum_scatter(dkeys, "seq", scatter_dimension=0, tiled=True)
    value_grad = lax.psum_scatter(dvalues, "seq", scatter_dimension=0, tiled=True)

    def weight_grad(grads):
        term = lax.dot_general(whole, grads, CONTRACT_FIRST, preferred_element_type=jnp.float32)
        return lax.psum_scatter(
            term.astype(jnp.bfloat16), "seq", scatter_dimension=0, tiled=True
        ).astype(jnp.float32)

    grad_w_query = weight_grad(grad_query)
    grad_kv = jnp.concatenate(
        [
            rotate(key_grad.astype(jnp.float32), cosine, sine, -1.0).astype(jnp.bfloat16),
            value_grad,
        ],
        axis=1,
    )
    term = lax.dot_general(
        grad_query, w_q, CONTRACT_LAST, preferred_element_type=jnp.float32
    ) + lax.dot_general(grad_kv, w_kv, CONTRACT_LAST, preferred_element_type=jnp.float32)
    grad_tokens = lax.psum_scatter(term.astype(jnp.bfloat16), "mp", scatter_dimension=1, tiled=True)
    grad_w_kv = weight_grad(grad_kv)
    return (grad_tokens, grad_w_query, grad_w_kv[:, :kv_cols], grad_w_kv[:, kv_cols:])


def solution(mesh):
    placed = (P("seq", "mp"), P("seq", "mp"), P("seq", "mp"), P("seq", "mp"), P("seq", "mp"), P())
    return jax.shard_map(
        local,
        mesh=mesh,
        in_specs=placed,
        out_specs=(P("seq", "mp"), P("seq", "mp"), P("seq", "mp"), P("seq", "mp")),
        check_vma=False,
    )
```

```python
import functools

import jax
import jax.numpy as jnp
from jax import lax
from jax.experimental import pallas as pl
from jax.experimental.pallas import tpu as pltpu
from jax.sharding import PartitionSpec as P

HEAD_DIM = 128
WINDOW = 4096
ALIGN = 128
THETA = 10000.0
KEY_BLOCK = 256
LOG2E = 1.4426950408889634
CONTRACT_LAST = (((1,), (1,)), ((), ()))
CONTRACT_FIRST = (((0,), (0,)), ((), ()))


def list_starts(positions, lengths):
    start = jnp.zeros_like(positions)
    end = jnp.int32(0)
    for k in range(lengths.shape[0]):
        end = end + lengths[k] * ALIGN
        start = jnp.where(positions >= end, end, start)
    return start


def rope_tables(offsets):
    half = HEAD_DIM // 2
    inverse = THETA ** (-(jnp.arange(half, dtype=jnp.float32) * 2.0 / HEAD_DIM))
    angle = offsets.astype(jnp.float32)[:, None] * inverse[None, :]
    cosine, sine = jnp.cos(angle), jnp.sin(angle)
    return (
        jnp.concatenate([cosine, cosine], axis=1),
        jnp.concatenate([-sine, sine], axis=1),
    )


def rotate(flat, cosine, sine, direction):
    half = HEAD_DIM // 2
    out = []
    for h in range(flat.shape[1] // HEAD_DIM):
        v = flat[:, h * HEAD_DIM : (h + 1) * HEAD_DIM]
        turned = jnp.concatenate([v[:, half:], v[:, :half]], axis=1)
        out.append(v * cosine + direction * turned * sine)
    return jnp.concatenate(out, axis=1)


def attention_kernel(
    group, scale, span_ref, q_ref, go_ref, k_ref, v_ref, cos_ref, sin_ref, low_ref, pos_ref,
    dq_ref, dkv_ref, score_ref, gprob_ref, dqt_ref,
):
    half = HEAD_DIM // 2
    kb = KEY_BLOCK
    rows = q_ref.shape[0]
    cols = group * rows
    first_block, blocks = span_ref[0], span_ref[1]
    cosine, sine = cos_ref[...], sin_ref[...]

    def head(ref, h):
        return ref[:, h * HEAD_DIM : (h + 1) * HEAD_DIM]

    query = jnp.concatenate(
        [
            (head(q_ref, h) * cosine + pltpu.roll(head(q_ref, h), half, 1) * sine).astype(jnp.bfloat16)
            for h in range(group)
        ],
        axis=0,
    )
    grads = jnp.concatenate([head(go_ref, h) for h in range(group)], axis=0)
    low = jnp.concatenate([low_ref[...]] * group, axis=1)
    pos = jnp.concatenate([pos_ref[...]] * group, axis=1)
    dkv_ref[...] = jnp.zeros_like(dkv_ref)
    dqt_ref[...] = jnp.zeros_like(dqt_ref)

    def rows_of(i):
        return pl.ds(pl.multiple_of((first_block + i) * kb, kb), kb)

    def fold(x, op):
        x = x.reshape(kb // 8, 8, cols)
        return op(x, axis=0)

    def score_step(i, top):
        s = lax.dot_general(
            k_ref[rows_of(i), :], query, CONTRACT_LAST, preferred_element_type=jnp.float32
        ) * (scale * LOG2E)
        kpos = (first_block + i) * kb + lax.broadcasted_iota(jnp.int32, (kb, cols), 0)
        s = jnp.where((kpos <= pos) & (kpos >= low), s, -jnp.inf)
        score_ref[i] = s
        return jnp.maximum(top, fold(s, jnp.max))

    top = lax.fori_loop(0, blocks, score_step, jnp.full((8, cols), -jnp.inf, jnp.float32))
    top = jnp.max(top, axis=0, keepdims=True)

    def mass_step(i, mass):
        e = jnp.exp2(score_ref[i] - top)
        score_ref[i] = e
        gprob_ref[i] = lax.dot_general(
            v_ref[rows_of(i), :], grads, CONTRACT_LAST, preferred_element_type=jnp.float32
        )
        return mass + fold(e, jnp.sum)

    mass = lax.fori_loop(0, blocks, mass_step, jnp.zeros((8, cols), jnp.float32))
    inverse = 1.0 / jnp.sum(mass, axis=0, keepdims=True)

    def delta_step(i, delta):
        low_probs = (score_ref[i] * inverse).astype(jnp.bfloat16)
        dkv_ref[rows_of(i), HEAD_DIM:] = jnp.dot(
            low_probs, grads, preferred_element_type=jnp.float32
        ).astype(dkv_ref.dtype)
        return delta + fold(low_probs.astype(jnp.float32) * gprob_ref[i], jnp.sum)

    delta = lax.fori_loop(0, blocks, delta_step, jnp.zeros((8, cols), jnp.float32))
    delta = jnp.sum(delta, axis=0, keepdims=True)

    def grad_step(i, carry):
        g = (score_ref[i] * inverse * (gprob_ref[i] - delta)).astype(jnp.bfloat16)
        dkv_ref[rows_of(i), :HEAD_DIM] = (
            jnp.dot(g, query, preferred_element_type=jnp.float32) * scale
        ).astype(dkv_ref.dtype)
        dqt_ref[...] += lax.dot_general(
            k_ref[rows_of(i), :], g, CONTRACT_FIRST, preferred_element_type=jnp.float32
        )
        return carry

    lax.fori_loop(0, blocks, grad_step, 0)
    for h in range(group):
        d = dqt_ref[:, h * rows : (h + 1) * rows].T * scale
        d = d * cosine - pltpu.roll(d, half, 1) * sine
        dq_ref[:, h * HEAD_DIM : (h + 1) * HEAD_DIM] = d.astype(dq_ref.dtype)


def attention(span, query, grad_out, keys_values, cosine, sine, low, pos):
    rows, head_cols = query.shape
    length, kv_cols = keys_values.shape[0], keys_values.shape[1] // 2
    kv_here = kv_cols // HEAD_DIM
    group = head_cols // kv_cols
    wide = group * HEAD_DIM
    cols = group * rows
    slots = min(length, WINDOW + rows) // KEY_BLOCK
    whole = lambda shape: pl.BlockSpec(shape, lambda g, s: (0, 0))
    column = pl.BlockSpec((length, HEAD_DIM), lambda g, s: (0, g))
    heads = pl.BlockSpec((rows, wide), lambda g, s: (0, g))
    return pl.pallas_call(
        functools.partial(attention_kernel, group, HEAD_DIM ** (-0.5)),
        grid_spec=pltpu.PrefetchScalarGridSpec(
            num_scalar_prefetch=1,
            grid=(kv_here,),
            in_specs=[
                heads,
                heads,
                column,
                pl.BlockSpec((length, HEAD_DIM), lambda g, s: (0, g + kv_here)),
                whole((rows, HEAD_DIM)),
                whole((rows, HEAD_DIM)),
                whole((1, rows)),
                whole((1, rows)),
            ],
            out_specs=[heads, pl.BlockSpec((length, 2 * HEAD_DIM), lambda g, s: (0, g))],
            scratch_shapes=[
                pltpu.VMEM((slots, KEY_BLOCK, cols), jnp.float32),
                pltpu.VMEM((slots, KEY_BLOCK, cols), jnp.float32),
                pltpu.VMEM((HEAD_DIM, cols), jnp.float32),
            ],
        ),
        out_shape=[
            jax.ShapeDtypeStruct((rows, head_cols), jnp.bfloat16),
            jax.ShapeDtypeStruct((length, 2 * kv_cols), jnp.bfloat16),
        ],
        compiler_params=pltpu.CompilerParams(vmem_limit_bytes=58 * 1024 * 1024),
        cost_estimate=pl.CostEstimate(
            flops=6 * rows * length * head_cols,
            bytes_accessed=8 * length * kv_cols,
            transcendentals=rows * length * head_cols // HEAD_DIM,
        ),
    )(span, query, grad_out, keys_values, keys_values, cosine, sine, low, pos)


def local(tokens, grad_out, w_query, w_key, w_value, doc_lengths):
    rows = tokens.shape[0]
    head_cols = w_query.shape[1]
    kv_cols = w_key.shape[1]
    first = lax.axis_index("seq") * rows
    pos = first + jnp.arange(rows, dtype=jnp.int32)
    start = list_starts(pos, doc_lengths)
    cosine, sine = rope_tables(pos - start)
    low = jnp.maximum(start, pos - (WINDOW - 1))
    first_block = low[0] // KEY_BLOCK
    blocks = (first + rows - 1) // KEY_BLOCK - first_block + 1
    span = jnp.stack([first_block, blocks]).astype(jnp.int32)

    pair = lax.axis_size("mp") == 2
    side = lax.axis_index("mp")
    swap = [(0, 1), (1, 0)]

    weights = lax.all_gather(
        jnp.concatenate([w_query, w_key, w_value], axis=1), "seq", axis=0, tiled=True
    )
    if pair:
        other = lax.ppermute(tokens, "mp", swap)
        whole = jnp.concatenate(
            [jnp.where(side == 0, tokens, other), jnp.where(side == 0, other, tokens)], axis=1
        )
    else:
        whole = lax.all_gather(tokens, "mp", axis=1, tiled=True)
    kv = jnp.dot(whole, weights[:, head_cols:], preferred_element_type=jnp.float32)
    keys_values = jnp.concatenate(
        [rotate(kv[:, :kv_cols], cosine, sine, 1.0).astype(jnp.bfloat16), kv[:, kv_cols:].astype(jnp.bfloat16)],
        axis=1,
    )
    keys_values = lax.all_gather(keys_values, "seq", axis=0, tiled=True)
    query = jnp.dot(whole, weights[:, :head_cols], preferred_element_type=jnp.float32)

    grad_query, dkeys_dvalues = attention(
        span, query, grad_out, keys_values, cosine, sine, low[None], pos[None]
    )
    dkeys_dvalues = lax.psum_scatter(dkeys_dvalues, "seq", scatter_dimension=0, tiled=True)
    pieces = [
        dkeys_dvalues[:, c : c + HEAD_DIM] for c in range(0, 2 * kv_cols, HEAD_DIM)
    ]
    key_grad = jnp.concatenate(pieces[0::2], axis=1).astype(jnp.float32)
    grad_all = jnp.concatenate(
        [grad_query, rotate(key_grad, cosine, sine, -1.0).astype(jnp.bfloat16)] + pieces[1::2],
        axis=1,
    )
    weight_term = lax.dot_general(
        whole, grad_all, CONTRACT_FIRST, preferred_element_type=jnp.float32
    )
    grad_weights = lax.psum_scatter(
        weight_term.astype(jnp.bfloat16), "seq", scatter_dimension=0, tiled=True
    ).astype(jnp.float32)
    term = lax.dot_general(grad_all, weights, CONTRACT_LAST, preferred_element_type=jnp.float32)
    if pair:
        width = tokens.shape[1]
        left, right = term[:, :width], term[:, width:]
        away = jnp.where(side == 0, right, left).astype(jnp.bfloat16)
        here = jnp.where(side == 0, left, right)
        grad_tokens = (here + lax.ppermute(away, "mp", swap).astype(jnp.float32)).astype(jnp.bfloat16)
    else:
        grad_tokens = lax.psum_scatter(
            term.astype(jnp.bfloat16), "mp", scatter_dimension=1, tiled=True
        )
    return (
        grad_tokens,
        grad_weights[:, :head_cols],
        grad_weights[:, head_cols : head_cols + kv_cols],
        grad_weights[:, head_cols + kv_cols :],
    )


def solution(mesh):
    placed = (P("seq", "mp"), P("seq", "mp"), P("seq", "mp"), P("seq", "mp"), P("seq", "mp"), P())
    return jax.shard_map(
        local,
        mesh=mesh,
        in_specs=placed,
        out_specs=(P("seq", "mp"), P("seq", "mp"), P("seq", "mp"), P("seq", "mp")),
        check_vma=False,
    )
```
